128 devices in a mesh: row: 32 (over z_hi, x, y), col: 4 (over z_lo, core).
Axes of the slice: x: 4, y: 4, z: 4 (z_hi: 2, z_lo: 2; z = z_hi * 2 + z_lo), core: 2. Of those that a mesh axis runs over, the one named last changes fastest.
Arguments:
- pair_left: bfloat16 [4096, 384, 128], P('row', 'col'), may hold values from -6 to 6
- pair_right: bfloat16 [1024, 384, 128], P('col', 'row'), may hold values from -6 to 6
- pair_gate: bfloat16 [4096, 1024, 128], P('row', 'col'), may hold values from -6 to 6
- left_proj: bfloat16 [128, 128], replicated, may hold values from -0.5 to 0.5
- left_gate: bfloat16 [128, 128], replicated, may hold values from -0.5 to 0.5
- right_proj: bfloat16 [128, 128], replicated, may hold values from -0.5 to 0.5
- right_gate: bfloat16 [128, 128], replicated, may hold values from -0.5 to 0.5
- out_gate: bfloat16 [128, 128], replicated, may hold values from -0.5 to 0.5
- out_proj: bfloat16 [128, 128], replicated, may hold values from -0.5 to 0.5
Outputs:
- update: bfloat16 [4096, 1024, 128], P('row', 'col')
The draws below stay inside these ranges and needn't reach their ends.
All inputs are finite; a program needn't handle non-finite values.
Results may differ from the reference program's by a relative error of at most 0.0078.
Values may be sent and summed in bfloat16 or wider, within the bound.
No kernel may reach another device: no remote copies, remote signals or barrier semaphores. Data moves between devices by JAX's collectives and lax.ppermute only.
A program may use at most 256 MiB of HBM per device.

```python
import jax
import jax.numpy as jnp
from jax import lax

C = 128
ROW_DEV = 128
ROWS = 4096
COLS = 1024
KSUM = 384
N_ROW = 32


def level_of(own_key, dims, shards, low, high):
    gain = 1.0
    for axis_at, shards_of in shards:
        steps = jax.random.uniform(jax.random.fold_in(jax.random.fold_in(own_key, 6), axis_at), (shards_of,), jnp.float32, low / len(shards), high / len(shards))
        gain = gain * jnp.repeat(jnp.exp(steps), dims[axis_at] // shards_of).reshape((-1,) + (1,) * (len(dims) - 1 - axis_at))
    return gain


def gaussian(key, shape, scale, reach, split=(), held_as=jnp.bfloat16):
    factor_of = level_of(key, shape, split, -0.22, 0.18) if split else 1.0
    result = jax.random.normal(key, shape, jnp.float32) * scale * factor_of
    return jnp.minimum(jnp.maximum(result, -reach), reach).astype(held_as)


def setup_inputs(seed: int = 0) -> dict:
    streams_of = jax.random.split(jax.random.key(seed), 10)
    return {
        "pair_left": gaussian(streams_of[0], (ROWS, KSUM, C), 1.0, 6.0, ((0, 32), (1, 4))),
        "pair_right": gaussian(streams_of[1], (COLS, KSUM, C), 1.0, 6.0, ((0, 4), (1, 32))),
        "pair_gate": gaussian(streams_of[2], (ROWS, COLS, C), 1.0, 6.0, ((0, 32), (1, 4))),
        "left_proj": gaussian(streams_of[3], (C, C), C ** -0.5, 0.5),
        "left_gate": gaussian(streams_of[4], (C, C), C ** -0.5, 0.5),
        "right_proj": gaussian(streams_of[5], (C, C), C ** -0.5, 0.5),
        "right_gate": gaussian(streams_of[6], (C, C), C ** -0.5, 0.5),
        "out_gate": gaussian(streams_of[7], (C, C), C ** -0.5, 0.5),
        "out_proj": gaussian(streams_of[8], (C, C), C ** -0.5, 0.5),
    }


epsilon = 1e-05

def normalize(values):
    floats = values.astype(jnp.float32)
    average = lax.optimization_barrier(jnp.mean(floats, axis=-1, keepdims=True))
    variance = lax.optimization_barrier(jnp.mean(jnp.square(floats - average), axis=-1, keepdims=True))
    return ((floats - average) * lax.rsqrt(variance + epsilon)).astype(jnp.bfloat16)

def project(pair, proj_weight, gate_weight):
    normed = normalize(pair)
    linear = jnp.dot(normed, proj_weight, preferred_element_type=jnp.float32)
    logits = jnp.dot(normed, gate_weight, preferred_element_type=jnp.float32)
    return (jax.nn.sigmoid(logits) * linear).astype(jnp.bfloat16)

def reference(pair_left, pair_right, pair_gate, left_proj, left_gate, right_proj, right_gate, out_gate, out_proj):
    right_value = project(pair_right, right_proj, right_gate).astype(jnp.float32)
    left_blocks = pair_left.reshape(N_ROW, ROW_DEV, KSUM, C)
    gate_blocks = pair_gate.reshape(N_ROW, ROW_DEV, COLS, C)

    def one_block(inputs):
        left_block, gate_block = inputs
        left_value = project(left_block, left_proj, left_gate).astype(jnp.float32)
        combined = jnp.einsum('ikc,jkc->ijc', left_value, right_value)
        combined_normed = normalize(combined)
        mixed = jnp.dot(combined_normed, out_proj, preferred_element_type=jnp.float32)
        gate_normed = normalize(gate_block)
        logits = jnp.dot(gate_normed, out_gate, preferred_element_type=jnp.float32)
        return (jax.nn.sigmoid(logits) * mixed).astype(jnp.bfloat16)
    blocks = lax.map(one_block, (left_blocks, gate_blocks))
    return blocks.reshape(ROWS, COLS, C)
```

```python
import functools

import jax
import jax.numpy as jnp
from jax import lax
from jax.experimental import pallas as pl
from jax.experimental.pallas import tpu as pltpu
from jax.sharding import PartitionSpec as P

epsilon = 1e-05
AXES = ("row", "col")
NX, NY, NZ = 4, 4, 4
VMEM_LIMIT = 56 * 1024 * 1024
CHANNELS = 128
SHORT = pl.CostEstimate(flops=1000, bytes_accessed=1000, transcendentals=0)


def device_index(x, y, z, core):
    return (((z // 2) * NX + x) * NY + y) * 4 + (z % 2) * 2 + core


def permutation(move):
    pairs = []
    for x in range(NX):
        for y in range(NY):
            for z in range(NZ):
                for core in range(2):
                    tx, ty, tz, tc = move(x, y, z, core)
                    pairs.append(
                        (
                            device_index(x, y, z, core),
                            device_index(tx % NX, ty % NY, tz % NZ, tc % 2),
                        )
                    )
    return pairs


RING_X = permutation(lambda x, y, z, c: (x + 1 - 2 * c, y, z, c))
RING_Y = permutation(lambda x, y, z, c: (x, y + 1 - 2 * c, z, c))
SWAP_Z_HI = permutation(lambda x, y, z, c: (x, y, z + 2, c))
SWAP_Z_LO = permutation(lambda x, y, z, c: (x, y, z + 1 - 2 * (z % 2), c))
SWAP_CORE = permutation(lambda x, y, z, c: (x, y, z, c + 1))


def normed_rows(values):
    floats = values.astype(jnp.float32)
    average = jnp.mean(floats, axis=-1, keepdims=True)
    centred = floats - average
    variance = jnp.mean(centred * centred, axis=-1, keepdims=True)
    return centred * lax.rsqrt(variance + epsilon)


def gated(both):
    return jax.nn.sigmoid(both[CHANNELS:]) * both[:CHANNELS]


def contract_last(a, b):
    return lax.dot_general(
        a, b, (((1,), (1,)), ((), ())), preferred_element_type=jnp.float32
    )


def both_weights(proj_ref, gate_ref):
    return jnp.concatenate([proj_ref[...].T, gate_ref[...].T], axis=0)


def left_kernel(x_ref, proj_ref, gate_ref, o_ref, rows, turned):
    n_i, n_k, _ = x_ref.shape
    rows[...] = normed_rows(x_ref[...]).reshape(n_i * n_k, CHANNELS)
    w = both_weights(proj_ref, gate_ref)
    for k in range(n_k):
        normed = rows[pl.ds(k, n_i, stride=n_k), :].astype(jnp.bfloat16)
        turned[pl.ds(k, CHANNELS, stride=n_k), :] = gated(contract_last(w, normed))
    o_ref[...] = turned[...].reshape(CHANNELS, n_k, n_i).astype(jnp.bfloat16)


def project_left(pair, proj, gate):
    n_i, n_k, _ = pair.shape
    block = 16
    return pl.pallas_call(
        left_kernel,
        grid=(n_k // block,),
        in_specs=[
            pl.BlockSpec((n_i, block, CHANNELS), lambda s: (0, s, 0)),
            pl.BlockSpec((CHANNELS, CHANNELS), lambda s: (0, 0)),
            pl.BlockSpec((CHANNELS, CHANNELS), lambda s: (0, 0)),
        ],
        out_specs=pl.BlockSpec((CHANNELS, block, n_i), lambda s: (0, s, 0)),
        out_shape=jax.ShapeDtypeStruct((CHANNELS, n_k, n_i), jnp.bfloat16),
        scratch_shapes=[
            pltpu.VMEM((n_i * block, CHANNELS), jnp.float32),
            pltpu.VMEM((CHANNELS * block, n_i), jnp.float32),
        ],
        compiler_params=pltpu.CompilerParams(vmem_limit_bytes=VMEM_LIMIT),
        cost_estimate=SHORT,
        name="project_left",
    )(pair, proj, gate)


def right_kernel(own_ref, other_ref, proj_ref, gate_ref, x_out, y_out, turned):
    n_k, n_j, _ = own_ref.shape
    w = both_weights(proj_ref, gate_ref)
    for at, ref in ((0, own_ref), (n_k, other_ref)):
        normed = normed_rows(ref[...]).astype(jnp.bfloat16)
        for k in range(n_k):
            turned[pl.ds(at + k, CHANNELS, stride=2 * n_k), :] = gated(contract_last(w, normed[k]))
    half = CHANNELS // 2
    whole = turned[...].reshape(CHANNELS, 2 * n_k, n_j).astype(jnp.bfloat16)
    x_out[...] = whole[:half]
    y_out[...] = whole[half:]


def project_right(own, other, proj, gate):
    n_k, n_j, _ = own.shape
    half = jax.ShapeDtypeStruct((CHANNELS // 2, 2 * n_k, n_j), jnp.bfloat16)
    return pl.pallas_call(
        right_kernel,
        out_shape=(half, half),
        scratch_shapes=[pltpu.VMEM((CHANNELS * 2 * n_k, n_j), jnp.float32)],
        compiler_params=pltpu.CompilerParams(vmem_limit_bytes=VMEM_LIMIT),
        cost_estimate=SHORT,
        name="project_right",
    )(own, other, proj, gate)


def gate_kernel(x_ref, w_ref, o_ref):
    n_i, n_j, _ = x_ref.shape
    normed = normed_rows(x_ref[...]).reshape(n_i * n_j, CHANNELS).astype(jnp.bfloat16)
    logits = jnp.dot(normed, w_ref[...], preferred_element_type=jnp.float32)
    o_ref[...] = jax.nn.sigmoid(logits).reshape(n_i, n_j, CHANNELS).astype(jnp.bfloat16)


def gate_values(pair, weights, at, n_j):
    n_i = pair.shape[0]
    block = 16
    return pl.pallas_call(
        gate_kernel,
        grid=(n_i // block,),
        in_specs=[
            pl.BlockSpec((block, n_j, CHANNELS), lambda s: (s, at, 0)),
            pl.BlockSpec((CHANNELS, CHANNELS), lambda s: (0, 0)),
        ],
        out_specs=pl.BlockSpec((block, n_j, CHANNELS), lambda s: (s, 0, 0)),
        out_shape=jax.ShapeDtypeStruct((n_i, n_j, CHANNELS), jnp.bfloat16),
        compiler_params=pltpu.CompilerParams(vmem_limit_bytes=VMEM_LIMIT),
        cost_estimate=SHORT,
        name="gate_values",
    )(pair, weights)


def arrange_kernel(a_ref, b_ref, c_ref, d_ref, order_ref, *rest):
    o_ref = rest[-1]
    order = order_ref[0]
    for ch in range(o_ref.shape[0]):
        rows = jnp.concatenate([a_ref[ch], b_ref[ch], c_ref[ch], d_ref[ch]], axis=0)
        o_ref[ch] = lax.dot_general(
            rows, order, (((0,), (0,)), ((), ())), preferred_element_type=jnp.float32
        ).astype(jnp.bfloat16)


def arrange_left(parts, orders, first, whole=None):
    n_c, n_k, n_i = parts[0].shape
    block = 8
    depth = 4 * n_k
    steps = n_c // 2 // block
    in_specs = [pl.BlockSpec((block, n_k, n_i), lambda s: (s + first * steps, 0, 0))] * 4 + [
        pl.BlockSpec((1, depth, depth), lambda s: (first, 0, 0))
    ]
    operands = [*parts, orders]
    aliases = {}
    if whole is not None:
        in_specs.append(pl.BlockSpec(memory_space=pl.ANY))
        aliases = {len(operands): 0}
        operands.append(whole)
    return pl.pallas_call(
        arrange_kernel,
        grid=(steps,),
        in_specs=in_specs,
        out_specs=pl.BlockSpec((block, n_i, depth), lambda s: (s + first * steps, 0, 0)),
        out_shape=jax.ShapeDtypeStruct((n_c, n_i, depth), jnp.bfloat16),
        input_output_aliases=aliases,
        compiler_params=pltpu.CompilerParams(vmem_limit_bytes=VMEM_LIMIT),
        cost_estimate=SHORT,
        name="arrange_left",
    )(*operands)


def left_orders():
    row, col = lax.axis_index("row"), lax.axis_index("col")
    z_hi, x, y = row // 16, (row // 4) % 4, row % 4
    z_lo, core = col // 2, col % 2
    sign = 1 - 2 * core
    depth = 384
    k = lax.broadcasted_iota(jnp.int32, (depth, depth), 1)
    source = lax.broadcasted_iota(jnp.int32, (depth, depth), 0)
    second, first, z_rel, within = k // 96, (k // 24) % 4, (k // 12) % 2, k % 12
    z_abs = z_hi ^ z_rel

    def order(x_rel, y_rel):
        x_abs = (x - sign * x_rel) % 4
        y_abs = (y - sign * y_rel) % 4
        part = (z_abs ^ z_lo) * 2 + ((x_abs // 2) ^ core)
        return part * 96 + (x_abs % 2) * 48 + y_abs * 12 + within == source

    return jnp.stack([order(first, second), order(second, first)]).astype(jnp.bfloat16)


def update_kernel(n_sum, lx_ref, ly_ref, *refs):
    x_refs, y_refs, (s_ref, w_ref), (o_ref, combined) = refs[:4], refs[4:8], refs[8:10], refs[-2:]
    step = pl.program_id(0)

    @pl.when(step < n_sum)
    def _():
        n_c, n_i, _ = lx_ref.shape
        for at, l_ref, parts in ((0, lx_ref, x_refs), (CHANNELS // 2, ly_ref, y_refs)):
            for ch in range(n_c):
                right = jnp.concatenate([r[ch] for r in parts], axis=0)
                product = jnp.dot(l_ref[ch], right, preferred_element_type=jnp.float32)
                combined[pl.ds(at + step * n_c + ch, n_i, stride=CHANNELS), :] = product

    @pl.when(step >= n_sum)
    def _():
        block = o_ref.shape[0]
        w = w_ref[...]
        first = pl.multiple_of((step - n_sum) * block * CHANNELS, block * CHANNELS)
        for i in range(block):
            values = combined[pl.ds(first + i * CHANNELS, CHANNELS), :]
            average = jnp.mean(values, axis=0, keepdims=True)
            centred = values - average
            variance = jnp.mean(centred * centred, axis=0, keepdims=True)
            normed = (centred * lax.rsqrt(variance + epsilon)).astype(jnp.bfloat16)
            mixed = lax.dot_general(
                normed, w, (((0,), (0,)), ((), ())), preferred_element_type=jnp.float32
            )
            o_ref[i] = (mixed * s_ref[i].astype(jnp.float32)).astype(jnp.bfloat16)


def update_block(left, x_parts, y_parts, gate, weights, at, n_blocks, part, n_parts, whole=None):
    n_c, n_i, depth = left.shape
    half, n_k, n_j = x_parts[0].shape
    c_block, i_block = 16, 16
    rows = n_i // n_parts
    n_sum = half // c_block
    n_out = rows // i_block
    within = lambda s: jnp.minimum(s, n_sum - 1)
    out_at = lambda s: jnp.maximum(s - n_sum, 0) + part * n_out
    in_specs = (
        [
            pl.BlockSpec((c_block, rows, depth), lambda s: (within(s), part, 0)),
            pl.BlockSpec((c_block, rows, depth), lambda s: (within(s) + n_sum, part, 0)),
        ]
        + [pl.BlockSpec((c_block, n_k, n_j), lambda s: (within(s), 0, 0))] * 8
        + [
            pl.BlockSpec((i_block, n_j, CHANNELS), lambda s: (out_at(s), 0, 0)),
            pl.BlockSpec((CHANNELS, CHANNELS), lambda s: (0, 0)),
        ]
    )
    operands = [left, left, *x_parts, *y_parts, gate, weights]
    aliases = {}
    if whole is not None:
        in_specs.append(pl.BlockSpec(memory_space=pl.ANY))
        aliases = {len(operands): 0}
        operands.append(whole)
    return pl.pallas_call(
        functools.partial(update_kernel, n_sum),
        grid=(n_sum + n_out,),
        in_specs=in_specs,
        out_specs=pl.BlockSpec((i_block, n_j, CHANNELS), lambda s: (out_at(s), at, 0)),
        out_shape=jax.ShapeDtypeStruct((n_i, n_blocks * n_j, CHANNELS), jnp.bfloat16),
        scratch_shapes=[pltpu.VMEM((rows * CHANNELS, n_j), jnp.float32)],
        input_output_aliases=aliases,
        compiler_params=pltpu.CompilerParams(vmem_limit_bytes=VMEM_LIMIT),
        cost_estimate=SHORT,
        name="update_block",
    )(*operands)


def after(value, *others):
    return lax.optimization_barrier((value, *others))[0]


def step_on(pieces, rings, *others):
    ready = lax.optimization_barrier((*(held[-1] for held in pieces), *others))
    for held, ring, piece in zip(pieces, rings, ready):
        held.append(lax.ppermute(piece, AXES, ring))


def joined(pieces):
    return [[jnp.concatenate(held, axis=1)] for held in pieces]


def shards(
    pair_left,
    pair_right,
    pair_gate,
    left_proj,
    left_gate,
    right_proj,
    right_gate,
    out_gate,
    out_proj,
):
    right = jnp.transpose(pair_right, (1, 0, 2))
    n_j = 128
    n_blocks = right.shape[1] // n_j
    first_rings, second_rings = (RING_X, RING_Y), (RING_Y, RING_X)

    blocks = [right[:, b * n_j : (b + 1) * n_j] for b in range(n_blocks)]
    others = [lax.ppermute(block, AXES, SWAP_Z_HI) for block in blocks]
    left_local = project_left(pair_left, left_proj, left_gate)
    halves_0 = project_right(blocks[0], after(others[0], left_local), right_proj, right_gate)
    f0 = [[half] for half in halves_0]
    step_on(f0, first_rings)
    halves_1 = project_right(blocks[1], after(others[1], halves_0[0]), right_proj, right_gate)
    f1 = [[half] for half in halves_1]
    step_on(f1, first_rings)
    left_sent = after(left_local, others[1])
    left_far = lax.ppermute(left_sent, AXES, SWAP_Z_LO)
    step_on(f0, first_rings)
    step_on(f1, first_rings)
    step_on(f0, first_rings)
    step_on(f1, first_rings)
    c0 = joined(f0)
    step_on(c0, second_rings)
    c1 = joined(f1)
    step_on(c1, second_rings)
    gate_0 = gate_values(pair_gate, after(out_gate, c0[0][0], c0[1][0], c1[0][0], c1[1][0]), 0, n_j)
    left_core = lax.ppermute(after(left_local, f1[0][-1]), AXES, SWAP_CORE)
    step_on(c0, second_rings, gate_0)
    gate_1 = gate_values(pair_gate, after(out_gate, gate_0, c0[0][1], c0[1][1]), 1, n_j)
    left_far_core = lax.ppermute(after(left_far, gate_1), AXES, SWAP_CORE)
    parts = (left_local, left_core, left_far, left_far_core)
    orders = left_orders()
    left = arrange_left(parts, orders, 0)
    step_on(c0, second_rings, left)
    step_on(c1, second_rings, left, c0[0][2], c0[1][2])
    left = arrange_left(parts, after(orders, c0[0][2]), 1, left)
    whole = update_block(left, *c0, gate_0, out_proj, 0, n_blocks, 0, 2)
    step_on(c1, second_rings, whole)
    whole = update_block(
        left, *c0, gate_0, after(out_proj, c1[0][2], c1[1][2]), 0, n_blocks, 1, 2, whole
    )
    return update_block(left, *c1, gate_1, out_proj, 1, n_blocks, 0, 1, whole)


def solution(mesh):
    placed = (
        P("row", "col", None),
        P("col", "row", None),
        P("row", "col", None),
        P(),
        P(),
        P(),
        P(),
        P(),
        P(),
    )
    return jax.shard_map(
        shards, mesh=mesh, in_specs=placed, out_specs=P("row", "col", None), check_vma=False
    )
```

```python
import functools

import jax
import jax.numpy as jnp
from jax import lax
from jax.experimental import pallas as pl
from jax.experimental.pallas import tpu as pltpu
from jax.sharding import PartitionSpec as P

epsilon = 1e-05
AXES = ("row", "col")
NX, NY, NZ = 4, 4, 4
MIB = 1024 * 1024
CHANNELS = 128
SHORT = pl.CostEstimate(flops=1000, bytes_accessed=1000, transcendentals=0)


def device_index(x, y, z, core):
    return (((z // 2) * NX + x) * NY + y) * 4 + (z % 2) * 2 + core


def permutation(move):
    pairs = []
    for x in range(NX):
        for y in range(NY):
            for z in range(NZ):
                for core in range(2):
                    tx, ty, tz, tc = move(x, y, z, core)
                    pairs.append(
                        (
                            device_index(x, y, z, core),
                            device_index(tx % NX, ty % NY, tz % NZ, tc % 2),
                        )
                    )
    return pairs


RING_X = permutation(lambda x, y, z, c: (x + 1 - 2 * c, y, z, c))
RING_Y = permutation(lambda x, y, z, c: (x, y + 1 - 2 * c, z, c))
SWAP_Z_HI = permutation(lambda x, y, z, c: (x, y, z + 2, c))
SWAP_Z_LO = permutation(lambda x, y, z, c: (x, y, z + 1 - 2 * (z % 2), c))
SWAP_CORE = permutation(lambda x, y, z, c: (x, y, z, c + 1))


def normed_rows(values):
    floats = values.astype(jnp.float32)
    average = jnp.mean(floats, axis=-1, keepdims=True)
    centred = floats - average
    variance = jnp.mean(centred * centred, axis=-1, keepdims=True)
    return centred * lax.rsqrt(variance + epsilon)


def gated(both):
    return jax.nn.sigmoid(both[CHANNELS:]) * both[:CHANNELS]


def contract_last(a, b):
    return lax.dot_general(
        a, b, (((1,), (1,)), ((), ())), preferred_element_type=jnp.float32
    )


def both_weights(proj_ref, gate_ref):
    return jnp.concatenate([proj_ref[...].T, gate_ref[...].T], axis=0)


def left_kernel(x_ref, proj_ref, gate_ref, o_ref, rows, turned):
    n_i, n_k, _ = x_ref.shape
    rows[...] = normed_rows(x_ref[...]).reshape(n_i * n_k, CHANNELS)
    w = both_weights(proj_ref, gate_ref)
    for k in range(n_k):
        normed = rows[pl.ds(k, n_i, stride=n_k), :].astype(jnp.bfloat16)
        turned[pl.ds(k, CHANNELS, stride=n_k), :] = gated(contract_last(w, normed))
    o_ref[...] = turned[...].reshape(CHANNELS, n_k, n_i).astype(jnp.bfloat16)


def project_left(pair, proj, gate):
    n_i, n_k, _ = pair.shape
    block = 16
    return pl.pallas_call(
        left_kernel,
        grid=(n_k // block,),
        in_specs=[
            pl.BlockSpec((n_i, block, CHANNELS), lambda s: (0, s, 0)),
            pl.BlockSpec((CHANNELS, CHANNELS), lambda s: (0, 0)),
            pl.BlockSpec((CHANNELS, CHANNELS), lambda s: (0, 0)),
        ],
        out_specs=pl.BlockSpec((CHANNELS, block, n_i), lambda s: (0, s, 0)),
        out_shape=jax.ShapeDtypeStruct((CHANNELS, n_k, n_i), jnp.bfloat16),
        scratch_shapes=[
            pltpu.VMEM((n_i * block, CHANNELS), jnp.float32),
            pltpu.VMEM((CHANNELS * block, n_i), jnp.float32),
        ],
        compiler_params=pltpu.CompilerParams(vmem_limit_bytes=16 * MIB),
        cost_estimate=pl.CostEstimate(
            flops=2 * n_i * n_k * CHANNELS * 256,
            bytes_accessed=8 * n_i * n_k * CHANNELS,
            transcendentals=2 * n_i * n_k * CHANNELS,
        ),
        name="project_left",
    )(pair, proj, gate)


def right_kernel(own_ref, other_ref, proj_ref, gate_ref, x_out, y_out, turned):
    n_k, n_j, _ = own_ref.shape
    w = both_weights(proj_ref, gate_ref)
    for at, ref in ((0, own_ref), (n_k, other_ref)):
        normed = normed_rows(ref[...]).astype(jnp.bfloat16)
        for k in range(n_k):
            turned[pl.ds(at + k, CHANNELS, stride=2 * n_k), :] = gated(contract_last(w, normed[k]))
    half = CHANNELS // 2
    whole = turned[...].reshape(CHANNELS, 2 * n_k, n_j).astype(jnp.bfloat16)
    x_out[...] = whole[:half]
    y_out[...] = whole[half:]


def project_right(own, other, proj, gate):
    n_k, n_j, _ = own.shape
    half = jax.ShapeDtypeStruct((CHANNELS // 2, 2 * n_k, n_j), jnp.bfloat16)
    return pl.pallas_call(
        right_kernel,
        out_shape=(half, half),
        scratch_shapes=[pltpu.VMEM((CHANNELS * 2 * n_k, n_j), jnp.float32)],
        compiler_params=pltpu.CompilerParams(vmem_limit_bytes=16 * MIB),
        cost_estimate=SHORT,
        name="project_right",
    )(own, other, proj, gate)


def gate_kernel(x_ref, w_ref, o_ref):
    n_i, n_j, _ = x_ref.shape
    normed = normed_rows(x_ref[...]).reshape(n_i * n_j, CHANNELS).astype(jnp.bfloat16)
    logits = jnp.dot(normed, w_ref[...], preferred_element_type=jnp.float32)
    o_ref[...] = jax.nn.sigmoid(logits).reshape(n_i, n_j, CHANNELS).astype(jnp.bfloat16)


def gate_values(pair, weights, at, n_j):
    n_i = pair.shape[0]
    block = 16
    return pl.pallas_call(
        gate_kernel,
        grid=(n_i // block,),
        in_specs=[
            pl.BlockSpec((block, n_j, CHANNELS), lambda s: (s, at, 0)),
            pl.BlockSpec((CHANNELS, CHANNELS), lambda s: (0, 0)),
        ],
        out_specs=pl.BlockSpec((block, n_j, CHANNELS), lambda s: (s, 0, 0)),
        out_shape=jax.ShapeDtypeStruct((n_i, n_j, CHANNELS), jnp.bfloat16),
        compiler_params=pltpu.CompilerParams(vmem_limit_bytes=16 * MIB),
        cost_estimate=SHORT,
        name="gate_values",
    )(pair, weights)


def arrange_kernel(a_ref, b_ref, c_ref, d_ref, order_ref, *rest):
    o_ref = rest[-1]
    order = order_ref[0]
    for ch in range(o_ref.shape[0]):
        rows = jnp.concatenate([a_ref[ch], b_ref[ch], c_ref[ch], d_ref[ch]], axis=0)
        o_ref[ch] = lax.dot_general(
            rows, order, (((0,), (0,)), ((), ())), preferred_element_type=jnp.float32
        ).astype(jnp.bfloat16)


def arrange_left(near, near_core, far, far_core, orders, first, whole=None):
    n_c, n_k, n_i = near.shape
    block = 8
    depth = 4 * n_k
    steps = n_c // 2 // block
    in_specs = (
        [pl.BlockSpec((block, n_k, n_i), lambda s: (s + first * steps, 0, 0))] * 2
        + [pl.BlockSpec((block, n_k, n_i), lambda s: (s, 0, 0))] * 2
        + [pl.BlockSpec((1, depth, depth), lambda s: (first, 0, 0))]
    )
    operands = [near, near_core, far, far_core, orders]
    aliases = {}
    if whole is not None:
        in_specs.append(pl.BlockSpec(memory_space=pl.ANY))
        aliases = {len(operands): 0}
        operands.append(whole)
    return pl.pallas_call(
        arrange_kernel,
        grid=(steps,),
        in_specs=in_specs,
        out_specs=pl.BlockSpec((block, n_i, depth), lambda s: (s + first * steps, 0, 0)),
        out_shape=jax.ShapeDtypeStruct((n_c, n_i, depth), jnp.bfloat16),
        input_output_aliases=aliases,
        compiler_params=pltpu.CompilerParams(vmem_limit_bytes=12 * MIB),
        cost_estimate=SHORT,
        name="arrange_left",
    )(*operands)


def left_orders():
    row, col = lax.axis_index("row"), lax.axis_index("col")
    z_hi, x, y = row // 16, (row // 4) % 4, row % 4
    z_lo, core = col // 2, col % 2
    sign = 1 - 2 * core
    depth = 384
    k = lax.broadcasted_iota(jnp.int32, (depth, depth), 1)
    source = lax.broadcasted_iota(jnp.int32, (depth, depth), 0)
    second, first, z_rel, within = k // 96, (k // 24) % 4, (k // 12) % 2, k % 12
    z_abs = z_hi ^ z_rel

    def order(x_rel, y_rel):
        x_abs = (x - sign * x_rel) % 4
        y_abs = (y - sign * y_rel) % 4
        part = (z_abs ^ z_lo) * 2 + ((x_abs // 2) ^ core)
        return part * 96 + (x_abs % 2) * 48 + y_abs * 12 + within == source

    return jnp.stack([order(first, second), order(second, first)]).astype(jnp.bfloat16)


def update_kernel(n_sum, lx_ref, ly_ref, *refs):
    x_refs, y_refs, (s_ref, w_ref), (o_ref, combined) = refs[:4], refs[4:8], refs[8:10], refs[-2:]
    step = pl.program_id(0)

    @pl.when(step < n_sum)
    def _():
        n_c, n_i, _ = lx_ref.shape
        for at, l_ref, parts in ((0, lx_ref, x_refs), (CHANNELS // 2, ly_ref, y_refs)):
            for ch in range(n_c):
                right = jnp.concatenate([r[ch] for r in parts], axis=0)
                product = jnp.dot(l_ref[ch], right, preferred_element_type=jnp.float32)
                combined[pl.ds(at + step * n_c + ch, n_i, stride=CHANNELS), :] = product

    @pl.when(step >= n_sum)
    def _():
        block = o_ref.shape[0]
        w = w_ref[...]
        first = pl.multiple_of((step - n_sum) * block * CHANNELS, block * CHANNELS)
        for i in range(block):
            values = combined[pl.ds(first + i * CHANNELS, CHANNELS), :]
            average = jnp.mean(values, axis=0, keepdims=True)
            centred = values - average
            variance = jnp.mean(centred * centred, axis=0, keepdims=True)
            normed = (centred * lax.rsqrt(variance + epsilon)).astype(jnp.bfloat16)
            mixed = lax.dot_general(
                normed, w, (((0,), (0,)), ((), ())), preferred_element_type=jnp.float32
            )
            o_ref[i] = (mixed * s_ref[i].astype(jnp.float32)).astype(jnp.bfloat16)


def update_block(left, x_parts, y_parts, gate, weights, at, n_blocks, part, n_parts, whole=None):
    n_c, n_i, depth = left.shape
    half, n_k, n_j = x_parts[0].shape
    c_block, i_block = 16, 16
    rows = n_i // n_parts
    n_sum = half // c_block
    n_out = rows // i_block
    within = lambda s: jnp.minimum(s, n_sum - 1)
    out_at = lambda s: jnp.maximum(s - n_sum, 0) + part * n_out
    in_specs = (
        [
            pl.BlockSpec((c_block, rows, depth), lambda s: (within(s), part, 0)),
            pl.BlockSpec((c_block, rows, depth), lambda s: (within(s) + n_sum, part, 0)),
        ]
        + [pl.BlockSpec((c_block, n_k, n_j), lambda s: (within(s), 0, 0))] * 8
        + [
            pl.BlockSpec((i_block, n_j, CHANNELS), lambda s: (out_at(s), 0, 0)),
            pl.BlockSpec((CHANNELS, CHANNELS), lambda s: (0, 0)),
        ]
    )
    operands = [left, left, *x_parts, *y_parts, gate, weights]
    aliases = {}
    if whole is not None:
        in_specs.append(pl.BlockSpec(memory_space=pl.ANY))
        aliases = {len(operands): 0}
        operands.append(whole)
    return pl.pallas_call(
        functools.partial(update_kernel, n_sum),
        grid=(n_sum + n_out,),
        in_specs=in_specs,
        out_specs=pl.BlockSpec((i_block, n_j, CHANNELS), lambda s: (out_at(s), at, 0)),
        out_shape=jax.ShapeDtypeStruct((n_i, n_blocks * n_j, CHANNELS), jnp.bfloat16),
        scratch_shapes=[pltpu.VMEM((rows * CHANNELS, n_j), jnp.float32)],
        input_output_aliases=aliases,
        compiler_params=pltpu.CompilerParams(vmem_limit_bytes=30 * MIB),
        cost_estimate=SHORT,
        name="update_block",
    )(*operands)


def after(value, *others):
    return lax.optimization_barrier((value, *others))[0]


def step_on(pieces, rings, *others):
    ready = lax.optimization_barrier((*(held[-1] for held in pieces), *others))
    for held, ring, piece in zip(pieces, rings, ready):
        held.append(lax.ppermute(piece, AXES, ring))


def joined(pieces):
    return [[jnp.concatenate(held, axis=1)] for held in pieces]


def shards(
    pair_left,
    pair_right,
    pair_gate,
    left_proj,
    left_gate,
    right_proj,
    right_gate,
    out_gate,
    out_proj,
):
    right = jnp.transpose(pair_right, (1, 0, 2))
    n_j = 128
    n_blocks = right.shape[1] // n_j
    first_rings, second_rings = (RING_X, RING_Y), (RING_Y, RING_X)

    blocks = [right[:, b * n_j : (b + 1) * n_j] for b in range(n_blocks)]
    others = [lax.ppermute(block, AXES, SWAP_Z_HI) for block in blocks]
    left_local = project_left(pair_left, left_proj, left_gate)
    near = [left_local[: CHANNELS // 2], left_local[CHANNELS // 2 :]]
    halves_0 = project_right(blocks[0], after(others[0], left_local), right_proj, right_gate)
    f0 = [[half] for half in halves_0]
    step_on(f0, first_rings)
    near_core = lax.ppermute(after(left_local, *others), AXES, SWAP_CORE)
    far_0 = lax.ppermute(after(near[0], *others, *halves_0), AXES, SWAP_Z_LO)
    halves_1 = project_right(blocks[1], after(others[1], *halves_0), right_proj, right_gate)
    f1 = [[half] for half in halves_1]
    step_on(f1, first_rings)
    step_on(f0, first_rings, near_core, *halves_1)
    step_on(f1, first_rings, f0[0][1])
    step_on(f0, first_rings, f1[0][1], f1[1][1])
    step_on(f1, first_rings, f0[0][2], f0[1][2])

    c0 = joined(f0)
    step_on(c0, second_rings, f1[0][2], f1[1][2])
    c1 = joined(f1)
    step_on(c1, second_rings)
    step_on(c0, second_rings, far_0)
    far_1 = lax.ppermute(after(near[1], far_0), AXES, SWAP_Z_LO)
    gate_0 = gate_values(pair_gate, after(out_gate, c1[0][1], c1[1][1]), 0, n_j)
    far_core_0 = lax.ppermute(after(far_0, c1[0][1], c1[1][1]), AXES, SWAP_CORE)
    gate_1 = gate_values(pair_gate, after(out_gate, gate_0), 1, n_j)
    step_on(c0, second_rings, gate_1)
    step_on(c1, second_rings, c0[0][2], c0[1][2], gate_1)
    far_core_1 = lax.ppermute(after(far_1, c0[0][2], c0[1][2]), AXES, SWAP_CORE)
    orders = left_orders()
    left = arrange_left(
        left_local, near_core, far_0, far_core_0, after(orders, c0[0][2], c0[1][2]), 0
    )
    left = arrange_left(left_local, near_core, far_1, far_core_1, orders, 1, left)
    whole = update_block(left, *c0, gate_0, out_proj, 0, n_blocks, 0, 2)
    step_on(c1, second_rings, whole)
    whole = update_block(
        left, *c0, gate_0, after(out_proj, c1[0][2], c1[1][2]), 0, n_blocks, 1, 2, whole
    )
    return update_block(left, *c1, gate_1, out_proj, 1, n_blocks, 0, 1, whole)


def solution(mesh):
    placed = (
        P("row", "col", None),
        P("col", "row", None),
        P("row", "col", None),
        P(),
        P(),
        P(),
        P(),
        P(),
        P(),
    )
    return jax.shard_map(
        shards, mesh=mesh, in_specs=placed, out_specs=P("row", "col", None), check_vma=False
    )
```

```python
import functools

import jax
import jax.numpy as jnp
from jax import lax
from jax.experimental import pallas as pl
from jax.experimental.pallas import tpu as pltpu
from jax.sharding import PartitionSpec as P

epsilon = 1e-05
AXES = ("row", "col")
NX, NY, NZ = 4, 4, 4
MIB = 1024 * 1024
CHANNELS = 128
SHORT = pl.CostEstimate(flops=1000, bytes_accessed=1000, transcendentals=0)


def device_index(x, y, z, core):
    return (((z // 2) * NX + x) * NY + y) * 4 + (z % 2) * 2 + core


def permutation(move):
    pairs = []
    for x in range(NX):
        for y in range(NY):
            for z in range(NZ):
                for core in range(2):
                    tx, ty, tz, tc = move(x, y, z, core)
                    pairs.append(
                        (
                            device_index(x, y, z, core),
                            device_index(tx % NX, ty % NY, tz % NZ, tc % 2),
                        )
                    )
    return pairs


RING_X = permutation(lambda x, y, z, c: (x + 1 - 2 * c, y, z, c))
RING_Y = permutation(lambda x, y, z, c: (x, y + 1 - 2 * c, z, c))
SWAP_Z_HI = permutation(lambda x, y, z, c: (x, y, z + 2, c))
SWAP_Z_LO = permutation(lambda x, y, z, c: (x, y, z + 1 - 2 * (z % 2), c))
SWAP_CORE = permutation(lambda x, y, z, c: (x, y, z, c + 1))


def normed_rows(values):
    floats = values.astype(jnp.float32)
    average = jnp.mean(floats, axis=-1, keepdims=True)
    centred = floats - average
    variance = jnp.mean(centred * centred, axis=-1, keepdims=True)
    return centred * lax.rsqrt(variance + epsilon)


def gated(both):
    return jax.nn.sigmoid(both[CHANNELS:]) * both[:CHANNELS]


def contract_last(a, b):
    return lax.dot_general(
        a, b, (((1,), (1,)), ((), ())), preferred_element_type=jnp.float32
    )


def both_weights(proj_ref, gate_ref):
    return jnp.concatenate([proj_ref[...].T, gate_ref[...].T], axis=0)


def left_kernel(x_ref, proj_ref, gate_ref, o_ref, rows, turned):
    n_i, n_k, _ = x_ref.shape
    rows[...] = normed_rows(x_ref[...]).reshape(n_i * n_k, CHANNELS)
    w = both_weights(proj_ref, gate_ref)
    for k in range(n_k):
        normed = rows[pl.ds(k, n_i, stride=n_k), :].astype(jnp.bfloat16)
        turned[pl.ds(k, CHANNELS, stride=n_k), :] = gated(contract_last(w, normed))
    o_ref[...] = turned[...].reshape(CHANNELS, n_k, n_i).astype(jnp.bfloat16)


def project_left(pair, proj, gate):
    n_i, n_k, _ = pair.shape
    block = 16
    return pl.pallas_call(
        left_kernel,
        grid=(n_k // block,),
        in_specs=[
            pl.BlockSpec((n_i, block, CHANNELS), lambda s: (0, s, 0)),
            pl.BlockSpec((CHANNELS, CHANNELS), lambda s: (0, 0)),
            pl.BlockSpec((CHANNELS, CHANNELS), lambda s: (0, 0)),
        ],
        out_specs=pl.BlockSpec((CHANNELS, block, n_i), lambda s: (0, s, 0)),
        out_shape=jax.ShapeDtypeStruct((CHANNELS, n_k, n_i), jnp.bfloat16),
        scratch_shapes=[
            pltpu.VMEM((n_i * block, CHANNELS), jnp.float32),
            pltpu.VMEM((CHANNELS * block, n_i), jnp.float32),
        ],
        compiler_params=pltpu.CompilerParams(vmem_limit_bytes=16 * MIB),
        cost_estimate=pl.CostEstimate(
            flops=2 * n_i * n_k * CHANNELS * 256,
            bytes_accessed=8 * n_i * n_k * CHANNELS,
            transcendentals=2 * n_i * n_k * CHANNELS,
        ),
        name="project_left",
    )(pair, proj, gate)


def right_kernel(own_ref, other_ref, proj_ref, gate_ref, x_out, y_out, turned):
    n_k, n_j, _ = own_ref.shape
    w = both_weights(proj_ref, gate_ref)
    for at, ref in ((0, own_ref), (n_k, other_ref)):
        normed = normed_rows(ref[...]).astype(jnp.bfloat16)
        for k in range(n_k):
            turned[pl.ds(at + k, CHANNELS, stride=2 * n_k), :] = gated(contract_last(w, normed[k]))
    half = CHANNELS // 2
    whole = turned[...].reshape(CHANNELS, 2 * n_k, n_j).astype(jnp.bfloat16)
    x_out[...] = whole[:half]
    y_out[...] = whole[half:]


def project_right(own, other, proj, gate):
    n_k, n_j, _ = own.shape
    half = jax.ShapeDtypeStruct((CHANNELS // 2, 2 * n_k, n_j), jnp.bfloat16)
    return pl.pallas_call(
        right_kernel,
        out_shape=(half, half),
        scratch_shapes=[pltpu.VMEM((CHANNELS * 2 * n_k, n_j), jnp.float32)],
        compiler_params=pltpu.CompilerParams(vmem_limit_bytes=16 * MIB),
        cost_estimate=SHORT,
        name="project_right",
    )(own, other, proj, gate)


def gate_kernel(x_ref, w_ref, o_ref):
    n_i, n_j, _ = x_ref.shape
    normed = normed_rows(x_ref[...]).reshape(n_i * n_j, CHANNELS).astype(jnp.bfloat16)
    logits = jnp.dot(normed, w_ref[...], preferred_element_type=jnp.float32)
    o_ref[...] = jax.nn.sigmoid(logits).reshape(n_i, n_j, CHANNELS).astype(jnp.bfloat16)


def gate_values(pair, weights, at, n_j):
    n_i = pair.shape[0]
    block = 16
    return pl.pallas_call(
        gate_kernel,
        grid=(n_i // block,),
        in_specs=[
            pl.BlockSpec((block, n_j, CHANNELS), lambda s: (s, at, 0)),
            pl.BlockSpec((CHANNELS, CHANNELS), lambda s: (0, 0)),
        ],
        out_specs=pl.BlockSpec((block, n_j, CHANNELS), lambda s: (s, 0, 0)),
        out_shape=jax.ShapeDtypeStruct((n_i, n_j, CHANNELS), jnp.bfloat16),
        compiler_params=pltpu.CompilerParams(vmem_limit_bytes=16 * MIB),
        cost_estimate=SHORT,
        name="gate_values",
    )(pair, weights)


def arrange_kernel(a_ref, b_ref, c_ref, d_ref, order_ref, *rest):
    o_ref = rest[-1]
    order = order_ref[0]
    for ch in range(o_ref.shape[0]):
        rows = jnp.concatenate([a_ref[ch], b_ref[ch], c_ref[ch], d_ref[ch]], axis=0)
        o_ref[ch] = lax.dot_general(
            rows, order, (((0,), (0,)), ((), ())), preferred_element_type=jnp.float32
        ).astype(jnp.bfloat16)


def arrange_left(near, near_core, far, far_core, orders, first, whole=None):
    n_c, n_k, n_i = near.shape
    block = 8
    depth = 4 * n_k
    steps = n_c // 2 // block
    in_specs = (
        [pl.BlockSpec((block, n_k, n_i), lambda s: (s + first * steps, 0, 0))] * 2
        + [pl.BlockSpec((block, n_k, n_i), lambda s: (s, 0, 0))] * 2
        + [pl.BlockSpec((1, depth, depth), lambda s: (first, 0, 0))]
    )
    operands = [near, near_core, far, far_core, orders]
    aliases = {}
    if whole is not None:
        in_specs.append(pl.BlockSpec(memory_space=pl.ANY))
        aliases = {len(operands): 0}
        operands.append(whole)
    return pl.pallas_call(
        arrange_kernel,
        grid=(steps,),
        in_specs=in_specs,
        out_specs=pl.BlockSpec((block, n_i, depth), lambda s: (s + first * steps, 0, 0)),
        out_shape=jax.ShapeDtypeStruct((n_c, n_i, depth), jnp.bfloat16),
        input_output_aliases=aliases,
        compiler_params=pltpu.CompilerParams(vmem_limit_bytes=12 * MIB),
        cost_estimate=SHORT,
        name="arrange_left",
    )(*operands)


def left_orders():
    row, col = lax.axis_index("row"), lax.axis_index("col")
    z_hi, x, y = row // 16, (row // 4) % 4, row % 4
    z_lo, core = col // 2, col % 2
    sign = 1 - 2 * core
    depth = 384
    k = lax.broadcasted_iota(jnp.int32, (depth, depth), 1)
    source = lax.broadcasted_iota(jnp.int32, (depth, depth), 0)
    second, first, z_rel, within = k // 96, (k // 24) % 4, (k // 12) % 2, k % 12
    z_abs = z_hi ^ z_rel

    def order(x_rel, y_rel):
        x_abs = (x - sign * x_rel) % 4
        y_abs = (y - sign * y_rel) % 4
        part = (z_abs ^ z_lo) * 2 + ((x_abs // 2) ^ core)
        return part * 96 + (x_abs % 2) * 48 + y_abs * 12 + within == source

    return jnp.stack([order(first, second), order(second, first)]).astype(jnp.bfloat16)


def update_kernel(n_sum, lx_ref, ly_ref, *refs):
    x_refs, y_refs, (s_ref, w_ref), (o_ref, combined) = refs[:4], refs[4:8], refs[8:10], refs[-2:]
    step = pl.program_id(0)

    @pl.when(step < n_sum)
    def _():
        n_c, n_i, _ = lx_ref.shape
        for at, l_ref, parts in ((0, lx_ref, x_refs), (CHANNELS // 2, ly_ref, y_refs)):
            for ch in range(n_c):
                right = jnp.concatenate([r[ch] for r in parts], axis=0)
                product = jnp.dot(l_ref[ch], right, preferred_element_type=jnp.float32)
                combined[pl.ds(at + step * n_c + ch, n_i, stride=CHANNELS), :] = product

    @pl.when(step >= n_sum)
    def _():
        block = o_ref.shape[0]
        w = w_ref[...]
        first = pl.multiple_of((step - n_sum) * block * CHANNELS, block * CHANNELS)
        for i in range(block):
            values = combined[pl.ds(first + i * CHANNELS, CHANNELS), :]
            average = jnp.mean(values, axis=0, keepdims=True)
            centred = values - average
            variance = jnp.mean(centred * centred, axis=0, keepdims=True)
            normed = (centred * lax.rsqrt(variance + epsilon)).astype(jnp.bfloat16)
            mixed = lax.dot_general(
                normed, w, (((0,), (0,)), ((), ())), preferred_element_type=jnp.float32
            )
            o_ref[i] = (mixed * s_ref[i].astype(jnp.float32)).astype(jnp.bfloat16)


def update_block(left, x_parts, y_parts, gate, weights, at, n_blocks, part, n_parts, whole=None):
    n_c, n_i, depth = left.shape
    half, n_k, n_j = x_parts[0].shape
    c_block, i_block = 16, 16
    rows = n_i // n_parts
    n_sum = half // c_block
    n_out = rows // i_block
    within = lambda s: jnp.minimum(s, n_sum - 1)
    out_at = lambda s: jnp.maximum(s - n_sum, 0) + part * n_out
    in_specs = (
        [
            pl.BlockSpec((c_block, rows, depth), lambda s: (within(s), part, 0)),
            pl.BlockSpec((c_block, rows, depth), lambda s: (within(s) + n_sum, part, 0)),
        ]
        + [pl.BlockSpec((c_block, n_k, n_j), lambda s: (within(s), 0, 0))] * 8
        + [
            pl.BlockSpec((i_block, n_j, CHANNELS), lambda s: (out_at(s), 0, 0)),
            pl.BlockSpec((CHANNELS, CHANNELS), lambda s: (0, 0)),
        ]
    )
    operands = [left, left, *x_parts, *y_parts, gate, weights]
    aliases = {}
    if whole is not None:
        in_specs.append(pl.BlockSpec(memory_space=pl.ANY))
        aliases = {len(operands): 0}
        operands.append(whole)
    return pl.pallas_call(
        functools.partial(update_kernel, n_sum),
        grid=(n_sum + n_out,),
        in_specs=in_specs,
        out_specs=pl.BlockSpec((i_block, n_j, CHANNELS), lambda s: (out_at(s), at, 0)),
        out_shape=jax.ShapeDtypeStruct((n_i, n_blocks * n_j, CHANNELS), jnp.bfloat16),
        scratch_shapes=[pltpu.VMEM((rows * CHANNELS, n_j), jnp.float32)],
        input_output_aliases=aliases,
        compiler_params=pltpu.CompilerParams(vmem_limit_bytes=30 * MIB),
        cost_estimate=SHORT,
        name="update_block",
    )(*operands)


def after(value, *others):
    return lax.optimization_barrier((value, *others))[0]


def step_on(pieces, rings, *others):
    ready = lax.optimization_barrier((*(held[-1] for held in pieces), *others))
    for held, ring, piece in zip(pieces, rings, ready):
        held.append(lax.ppermute(piece, AXES, ring))


def joined(pieces):
    return [[jnp.concatenate(held, axis=1)] for held in pieces]


def shards(
    pair_left,
    pair_right,
    pair_gate,
    left_proj,
    left_gate,
    right_proj,
    right_gate,
    out_gate,
    out_proj,
):
    right = jnp.transpose(pair_right, (1, 0, 2))
    n_j = 128
    n_blocks = right.shape[1] // n_j
    first_rings, second_rings = (RING_X, RING_Y), (RING_Y, RING_X)

    blocks = [right[:, b * n_j : (b + 1) * n_j] for b in range(n_blocks)]
    others = [lax.ppermute(block, AXES, SWAP_Z_HI) for block in blocks]
    left_local = project_left(pair_left, left_proj, left_gate)
    near = [left_local[: CHANNELS // 2], left_local[CHANNELS // 2 :]]
    halves_0 = project_right(blocks[0], after(others[0], left_local), right_proj, right_gate)
    f0 = [[half] for half in halves_0]
    step_on(f0, first_rings)
    near_core = lax.ppermute(after(left_local, *others), AXES, SWAP_CORE)
    far_0 = lax.ppermute(after(near[0], *others, *halves_0), AXES, SWAP_Z_LO)
    halves_1 = project_right(blocks[1], after(others[1], *halves_0), right_proj, right_gate)
    f1 = [[half] for half in halves_1]
    step_on(f1, first_rings)
    step_on(f0, first_rings, near_core, *halves_1)
    step_on(f1, first_rings, f0[0][1])
    step_on(f0, first_rings, f1[0][1], f1[1][1])
    step_on(f1, first_rings, f0[0][2], f0[1][2])

    c0 = joined(f0)
    step_on(c0, second_rings, f1[0][2], f1[1][2])
    c1 = joined(f1)
    step_on(c1, second_rings)
    step_on(c0, second_rings, far_0)
    far_core_0 = lax.ppermute(after(far_0, f1[0][3], f1[1][3]), AXES, SWAP_CORE)
    far_1 = lax.ppermute(after(near[1], far_core_0), AXES, SWAP_Z_LO)
    gate_0 = gate_values(pair_gate, after(out_gate, c0[0][1], c0[1][1], far_core_0), 0, n_j)
    orders = left_orders()
    left = arrange_left(left_local, near_core, far_0, far_core_0, after(orders, gate_0), 0)
    gate_1 = gate_values(pair_gate, after(out_gate, left, c1[0][1], c1[1][1]), 1, n_j)
    step_on(c1, second_rings, gate_1)
    step_on(c0, second_rings, gate_1)
    far_core_1 = lax.ppermute(after(far_1, c0[0][2], c0[1][2]), AXES, SWAP_CORE)
    left = arrange_left(
        left_local, near_core, far_1, far_core_1, after(orders, c0[0][2], c0[1][2]), 1, left
    )
    step_on(c1, second_rings, left)
    whole = update_block(left, *c0, gate_0, out_proj, 0, n_blocks, 0, 1)
    return update_block(left, *c1, gate_1, out_proj, 1, n_blocks, 0, 1, whole)


def solution(mesh):
    placed = (
        P("row", "col", None),
        P("col", "row", None),
        P("row", "col", None),
        P(),
        P(),
        P(),
        P(),
        P(),
        P(),
    )
    return jax.shard_map(
        shards, mesh=mesh, in_specs=placed, out_specs=P("row", "col", None), check_vma=False
    )
```

```python
import functools

import jax
import jax.numpy as jnp
from jax import lax
from jax.experimental import pallas as pl
from jax.experimental.pallas import tpu as pltpu
from jax.sharding import PartitionSpec as P

epsilon = 1e-05
AXES = ("row", "col")
NX, NY, NZ = 4, 4, 4
MIB = 1024 * 1024
CHANNELS = 128
SHORT = pl.CostEstimate(flops=1000, bytes_accessed=1000, transcendentals=0)


def device_index(x, y, z, core):
    return (((z // 2) * NX + x) * NY + y) * 4 + (z % 2) * 2 + core


def permutation(move):
    pairs = []
    for x in range(NX):
        for y in range(NY):
            for z in range(NZ):
                for core in range(2):
                    tx, ty, tz, tc = move(x, y, z, core)
                    pairs.append(
                        (
                            device_index(x, y, z, core),
                            device_index(tx % NX, ty % NY, tz % NZ, tc % 2),
                        )
                    )
    return pairs


RING_X = permutation(lambda x, y, z, c: (x + 1 - 2 * c, y, z, c))
RING_Y = permutation(lambda x, y, z, c: (x, y + 1 - 2 * c, z, c))
SWAP_Z_HI = permutation(lambda x, y, z, c: (x, y, z + 2, c))
SWAP_Z_LO = permutation(lambda x, y, z, c: (x, y, z + 1 - 2 * (z % 2), c))
SWAP_CORE = permutation(lambda x, y, z, c: (x, y, z, c + 1))


def normed_rows(values):
    floats = values.astype(jnp.float32)
    average = jnp.mean(floats, axis=-1, keepdims=True)
    centred = floats - average
    variance = jnp.mean(centred * centred, axis=-1, keepdims=True)
    return centred * lax.rsqrt(variance + epsilon)


def gated(both):
    return jax.nn.sigmoid(both[CHANNELS:]) * both[:CHANNELS]


def contract_last(a, b):
    return lax.dot_general(
        a, b, (((1,), (1,)), ((), ())), preferred_element_type=jnp.float32
    )


def both_weights(proj_ref, gate_ref):
    return jnp.concatenate([proj_ref[...].T, gate_ref[...].T], axis=0)


def left_kernel(x_ref, proj_ref, gate_ref, o_ref, rows, turned):
    n_i, n_k, _ = x_ref.shape
    rows[...] = normed_rows(x_ref[...]).reshape(n_i * n_k, CHANNELS)
    w = both_weights(proj_ref, gate_ref)
    for k in range(n_k):
        normed = rows[pl.ds(k, n_i, stride=n_k), :].astype(jnp.bfloat16)
        turned[pl.ds(k, CHANNELS, stride=n_k), :] = gated(contract_last(w, normed))
    o_ref[...] = turned[...].reshape(CHANNELS, n_k, n_i).astype(jnp.bfloat16)


def project_left(pair, proj, gate):
    n_i, n_k, _ = pair.shape
    block = 16
    return pl.pallas_call(
        left_kernel,
        grid=(n_k // block,),
        in_specs=[
            pl.BlockSpec((n_i, block, CHANNELS), lambda s: (0, s, 0)),
            pl.BlockSpec((CHANNELS, CHANNELS), lambda s: (0, 0)),
            pl.BlockSpec((CHANNELS, CHANNELS), lambda s: (0, 0)),
        ],
        out_specs=pl.BlockSpec((CHANNELS, block, n_i), lambda s: (0, s, 0)),
        out_shape=jax.ShapeDtypeStruct((CHANNELS, n_k, n_i), jnp.bfloat16),
        scratch_shapes=[
            pltpu.VMEM((n_i * block, CHANNELS), jnp.float32),
            pltpu.VMEM((CHANNELS * block, n_i), jnp.float32),
        ],
        compiler_params=pltpu.CompilerParams(vmem_limit_bytes=16 * MIB),
        cost_estimate=pl.CostEstimate(
            flops=2 * n_i * n_k * CHANNELS * 256,
            bytes_accessed=8 * n_i * n_k * CHANNELS,
            transcendentals=2 * n_i * n_k * CHANNELS,
        ),
        name="project_left",
    )(pair, proj, gate)


def right_kernel(own_ref, other_ref, proj_ref, gate_ref, x_out, y_out, turned):
    n_k, n_j, _ = own_ref.shape
    w = both_weights(proj_ref, gate_ref)
    for at, ref in ((0, own_ref), (n_k, other_ref)):
        normed = normed_rows(ref[...]).astype(jnp.bfloat16)
        for k in range(n_k):
            turned[pl.ds(at + k, CHANNELS, stride=2 * n_k), :] = gated(contract_last(w, normed[k]))
    half = CHANNELS // 2
    whole = turned[...].reshape(CHANNELS, 2 * n_k, n_j).astype(jnp.bfloat16)
    x_out[...] = whole[:half]
    y_out[...] = whole[half:]


def project_right(own, other, proj, gate):
    n_k, n_j, _ = own.shape
    half = jax.ShapeDtypeStruct((CHANNELS // 2, 2 * n_k, n_j), jnp.bfloat16)
    return pl.pallas_call(
        right_kernel,
        out_shape=(half, half),
        scratch_shapes=[pltpu.VMEM((CHANNELS * 2 * n_k, n_j), jnp.float32)],
        compiler_params=pltpu.CompilerParams(vmem_limit_bytes=16 * MIB),
        cost_estimate=SHORT,
        name="project_right",
    )(own, other, proj, gate)


def gate_kernel(x_ref, w_ref, o_ref):
    n_i, n_j, _ = x_ref.shape
    normed = normed_rows(x_ref[...]).reshape(n_i * n_j, CHANNELS).astype(jnp.bfloat16)
    logits = jnp.dot(normed, w_ref[...], preferred_element_type=jnp.float32)
    o_ref[...] = jax.nn.sigmoid(logits).reshape(n_i, n_j, CHANNELS).astype(jnp.bfloat16)


def gate_values(pair, weights, at, n_j):
    n_i = pair.shape[0]
    block = 16
    return pl.pallas_call(
        gate_kernel,
        grid=(n_i // block,),
        in_specs=[
            pl.BlockSpec((block, n_j, CHANNELS), lambda s: (s, at, 0)),
            pl.BlockSpec((CHANNELS, CHANNELS), lambda s: (0, 0)),
        ],
        out_specs=pl.BlockSpec((block, n_j, CHANNELS), lambda s: (s, 0, 0)),
        out_shape=jax.ShapeDtypeStruct((n_i, n_j, CHANNELS), jnp.bfloat16),
        compiler_params=pltpu.CompilerParams(vmem_limit_bytes=16 * MIB),
        cost_estimate=SHORT,
        name="gate_values",
    )(pair, weights)


def arrange_kernel(a_ref, b_ref, c_ref, d_ref, order_ref, *rest):
    o_ref = rest[-1]
    order = order_ref[0]
    for ch in range(o_ref.shape[0]):
        rows = jnp.concatenate([a_ref[ch], b_ref[ch], c_ref[ch], d_ref[ch]], axis=0)
        o_ref[ch] = lax.dot_general(
            rows, order, (((0,), (0,)), ((), ())), preferred_element_type=jnp.float32
        ).astype(jnp.bfloat16)


def arrange_left(near, near_core, far, far_core, orders, first, whole=None):
    n_c, n_k, n_i = near.shape
    block = 8
    depth = 4 * n_k
    steps = n_c // 2 // block
    in_specs = (
        [pl.BlockSpec((block, n_k, n_i), lambda s: (s + first * steps, 0, 0))] * 2
        + [pl.BlockSpec((block, n_k, n_i), lambda s: (s, 0, 0))] * 2
        + [pl.BlockSpec((1, depth, depth), lambda s: (first, 0, 0))]
    )
    operands = [near, near_core, far, far_core, orders]
    aliases = {}
    if whole is not None:
        in_specs.append(pl.BlockSpec(memory_space=pl.ANY))
        aliases = {len(operands): 0}
        operands.append(whole)
    return pl.pallas_call(
        arrange_kernel,
        grid=(steps,),
        in_specs=in_specs,
        out_specs=pl.BlockSpec((block, n_i, depth), lambda s: (s + first * steps, 0, 0)),
        out_shape=jax.ShapeDtypeStruct((n_c, n_i, depth), jnp.bfloat16),
        input_output_aliases=aliases,
        compiler_params=pltpu.CompilerParams(vmem_limit_bytes=12 * MIB),
        cost_estimate=SHORT,
        name="arrange_left",
    )(*operands)


def left_orders():
    row, col = lax.axis_index("row"), lax.axis_index("col")
    z_hi, x, y = row // 16, (row // 4) % 4, row % 4
    z_lo, core = col // 2, col % 2
    sign = 1 - 2 * core
    depth = 384
    k = lax.broadcasted_iota(jnp.int32, (depth, depth), 1)
    source = lax.broadcasted_iota(jnp.int32, (depth, depth), 0)
    second, first, z_rel, within = k // 96, (k // 24) % 4, (k // 12) % 2, k % 12
    z_abs = z_hi ^ z_rel

    def order(x_rel, y_rel):
        x_abs = (x - sign * x_rel) % 4
        y_abs = (y - sign * y_rel) % 4
        part = (z_abs ^ z_lo) * 2 + ((x_abs // 2) ^ core)
        return part * 96 + (x_abs % 2) * 48 + y_abs * 12 + within == source

    return jnp.stack([order(first, second), order(second, first)]).astype(jnp.bfloat16)


def update_kernel(n_sum, lx_ref, ly_ref, *refs):
    x_refs, y_refs, (s_ref, w_ref), (o_ref, combined) = refs[:4], refs[4:8], refs[8:10], refs[-2:]
    step = pl.program_id(0)

    @pl.when(step < n_sum)
    def _():
        n_c, n_i, _ = lx_ref.shape
        for at, l_ref, parts in ((0, lx_ref, x_refs), (CHANNELS // 2, ly_ref, y_refs)):
            for ch in range(n_c):
                right = jnp.concatenate([r[ch] for r in parts], axis=0)
                product = jnp.dot(l_ref[ch], right, preferred_element_type=jnp.float32)
                combined[pl.ds(at + step * n_c + ch, n_i, stride=CHANNELS), :] = product

    @pl.when(step >= n_sum)
    def _():
        block = o_ref.shape[0]
        w = w_ref[...]
        first = pl.multiple_of((step - n_sum) * block * CHANNELS, block * CHANNELS)
        for i in range(block):
            values = combined[pl.ds(first + i * CHANNELS, CHANNELS), :]
            average = jnp.mean(values, axis=0, keepdims=True)
            centred = values - average
            variance = jnp.mean(centred * centred, axis=0, keepdims=True)
            normed = (centred * lax.rsqrt(variance + epsilon)).astype(jnp.bfloat16)
            mixed = lax.dot_general(
                normed, w, (((0,), (0,)), ((), ())), preferred_element_type=jnp.float32
            )
            o_ref[i] = (mixed * s_ref[i].astype(jnp.float32)).astype(jnp.bfloat16)


def update_block(left, x_parts, y_parts, gate, weights, at, n_blocks, part, n_parts, whole=None):
    n_c, n_i, depth = left.shape
    half, n_k, n_j = x_parts[0].shape
    c_block, i_block = 16, 16
    rows = n_i // n_parts
    n_sum = half // c_block
    n_out = rows // i_block
    within = lambda s: jnp.minimum(s, n_sum - 1)
    out_at = lambda s: jnp.maximum(s - n_sum, 0) + part * n_out
    in_specs = (
        [
            pl.BlockSpec((c_block, rows, depth), lambda s: (within(s), part, 0)),
            pl.BlockSpec((c_block, rows, depth), lambda s: (within(s) + n_sum, part, 0)),
        ]
        + [pl.BlockSpec((c_block, n_k, n_j), lambda s: (within(s), 0, 0))] * 8
        + [
            pl.BlockSpec((i_block, n_j, CHANNELS), lambda s: (out_at(s), 0, 0)),
            pl.BlockSpec((CHANNELS, CHANNELS), lambda s: (0, 0)),
        ]
    )
    operands = [left, left, *x_parts, *y_parts, gate, weights]
    aliases = {}
    if whole is not None:
        in_specs.append(pl.BlockSpec(memory_space=pl.ANY))
        aliases = {len(operands): 0}
        operands.append(whole)
    return pl.pallas_call(
        functools.partial(update_kernel, n_sum),
        grid=(n_sum + n_out,),
        in_specs=in_specs,
        out_specs=pl.BlockSpec((i_block, n_j, CHANNELS), lambda s: (out_at(s), at, 0)),
        out_shape=jax.ShapeDtypeStruct((n_i, n_blocks * n_j, CHANNELS), jnp.bfloat16),
        scratch_shapes=[pltpu.VMEM((rows * CHANNELS, n_j), jnp.float32)],
        input_output_aliases=aliases,
        compiler_params=pltpu.CompilerParams(vmem_limit_bytes=30 * MIB),
        cost_estimate=SHORT,
        name="update_block",
    )(*operands)


def after(value, *others):
    return lax.optimization_barrier((value, *others))[0]


def step_on(pieces, rings, *others):
    ready = lax.optimization_barrier((*(held[-1] for held in pieces), *others))
    for held, ring, piece in zip(pieces, rings, ready):
        held.append(lax.ppermute(piece, AXES, ring))


def joined(pieces):
    return [[jnp.concatenate(held, axis=1)] for held in pieces]


def shards(
    pair_left,
    pair_right,
    pair_gate,
    left_proj,
    left_gate,
    right_proj,
    right_gate,
    out_gate,
    out_proj,
):
    right = jnp.transpose(pair_right, (1, 0, 2))
    n_j = 128
    n_blocks = right.shape[1] // n_j
    first_rings, second_rings = (RING_X, RING_Y), (RING_Y, RING_X)

    blocks = [right[:, b * n_j : (b + 1) * n_j] for b in range(n_blocks)]
    others = [lax.ppermute(block, AXES, SWAP_Z_HI) for block in blocks]
    left_local = project_left(pair_left, left_proj, left_gate)
    near = [left_local[: CHANNELS // 2], left_local[CHANNELS // 2 :]]
    halves_0 = project_right(blocks[0], after(others[0], left_local), right_proj, right_gate)
    f0 = [[half] for half in halves_0]
    step_on(f0, first_rings)
    halves_1 = project_right(blocks[1], after(others[1], *halves_0), right_proj, right_gate)
    near_core = lax.ppermute(after(left_local, *others, *halves_0), AXES, SWAP_CORE)
    far_0 = lax.ppermute(after(near[0], *halves_1), AXES, SWAP_Z_LO)
    f1 = [[half] for half in halves_1]
    step_on(f1, first_rings)
    step_on(f0, first_rings, *halves_1)
    step_on(f1, first_rings, f0[0][1])
    step_on(f0, first_rings, f1[0][1], f1[1][1], near_core)
    step_on(f1, first_rings, f0[0][2], f0[1][2])

    c0 = joined(f0)
    step_on(c0, second_rings, f1[0][3], f1[1][3])
    c1 = joined(f1)
    step_on(c1, second_rings)
    step_on(c0, second_rings, far_0)
    far_core_0 = lax.ppermute(after(far_0, *[h[3] for h in f1]), AXES, SWAP_CORE)
    far_1 = lax.ppermute(after(near[1], far_0), AXES, SWAP_Z_LO)
    gate_0 = gate_values(pair_gate, after(out_gate, c0[0][1], c0[1][1]), 0, n_j)
    orders = left_orders()
    left = arrange_left(left_local, near_core, far_0, far_core_0, after(orders, gate_0), 0)
    gate_1 = gate_values(pair_gate, after(out_gate, gate_0, c1[0][1], c1[1][1]), 1, n_j)
    step_on(c1, second_rings, gate_1)
    step_on(c0, second_rings)
    far_core_1 = lax.ppermute(after(far_1, c0[0][2], c0[1][2]), AXES, SWAP_CORE)
    left = arrange_left(left_local, near_core, far_1, far_core_1, after(orders, c0[0][2], c0[1][2]), 1, left)
    step_on(c1, second_rings, left)
    whole = update_block(left, *c0, gate_0, out_proj, 0, n_blocks, 0, 1)
    return update_block(left, *c1, gate_1, out_proj, 1, n_blocks, 0, 1, whole)


def solution(mesh):
    placed = (
        P("row", "col", None),
        P("col", "row", None),
        P("row", "col", None),
        P(),
        P(),
        P(),
        P(),
        P(),
        P(),
    )
    return jax.shard_map(
        shards, mesh=mesh, in_specs=placed, out_specs=P("row", "col", None), check_vma=False
    )
```

```python
import functools

import jax
import jax.numpy as jnp
from jax import lax
from jax.experimental import pallas as pl
from jax.experimental.pallas import tpu as pltpu
from jax.sharding import PartitionSpec as P

epsilon = 1e-05
AXES = ("row", "col")
NX, NY, NZ = 4, 4, 4
MIB = 1024 * 1024
CHANNELS = 128
SHORT = pl.CostEstimate(flops=1000, bytes_accessed=1000, transcendentals=0)


def device_index(x, y, z, core):
    return (((z // 2) * NX + x) * NY + y) * 4 + (z % 2) * 2 + core


def permutation(move):
    pairs = []
    for x in range(NX):
        for y in range(NY):
            for z in range(NZ):
                for core in range(2):
                    tx, ty, tz, tc = move(x, y, z, core)
                    pairs.append(
                        (
                            device_index(x, y, z, core),
                            device_index(tx % NX, ty % NY, tz % NZ, tc % 2),
                        )
                    )
    return pairs


RING_X = permutation(lambda x, y, z, c: (x + 1 - 2 * c, y, z, c))
RING_Y = permutation(lambda x, y, z, c: (x, y + 1 - 2 * c, z, c))
SWAP_Z_HI = permutation(lambda x, y, z, c: (x, y, z + 2, c))
SWAP_Z_LO = permutation(lambda x, y, z, c: (x, y, z + 1 - 2 * (z % 2), c))
SWAP_CORE = permutation(lambda x, y, z, c: (x, y, z, c + 1))


def normed_rows(values):
    floats = values.astype(jnp.float32)
    average = jnp.mean(floats, axis=-1, keepdims=True)
    centred = floats - average
    variance = jnp.mean(centred * centred, axis=-1, keepdims=True)
    return centred * lax.rsqrt(variance + epsilon)


def gated(both):
    return jax.nn.sigmoid(both[CHANNELS:]) * both[:CHANNELS]


def contract_last(a, b):
    return lax.dot_general(
        a, b, (((1,), (1,)), ((), ())), preferred_element_type=jnp.float32
    )


def both_weights(proj_ref, gate_ref):
    return jnp.concatenate([proj_ref[...].T, gate_ref[...].T], axis=0)


def left_kernel(x_ref, proj_ref, gate_ref, o_ref, rows, turned):
    n_i, n_k, _ = x_ref.shape
    rows[...] = normed_rows(x_ref[...]).reshape(n_i * n_k, CHANNELS)
    w = both_weights(proj_ref, gate_ref)
    for k in range(n_k):
        normed = rows[pl.ds(k, n_i, stride=n_k), :].astype(jnp.bfloat16)
        turned[pl.ds(k, CHANNELS, stride=n_k), :] = gated(contract_last(w, normed))
    o_ref[...] = turned[...].reshape(CHANNELS, n_k, n_i).astype(jnp.bfloat16)


def project_left(pair, proj, gate):
    n_i, n_k, _ = pair.shape
    block = 16
    return pl.pallas_call(
        left_kernel,
        grid=(n_k // block,),
        in_specs=[
            pl.BlockSpec((n_i, block, CHANNELS), lambda s: (0, s, 0)),
            pl.BlockSpec((CHANNELS, CHANNELS), lambda s: (0, 0)),
            pl.BlockSpec((CHANNELS, CHANNELS), lambda s: (0, 0)),
        ],
        out_specs=pl.BlockSpec((CHANNELS, block, n_i), lambda s: (0, s, 0)),
        out_shape=jax.ShapeDtypeStruct((CHANNELS, n_k, n_i), jnp.bfloat16),
        scratch_shapes=[
            pltpu.VMEM((n_i * block, CHANNELS), jnp.float32),
            pltpu.VMEM((CHANNELS * block, n_i), jnp.float32),
        ],
        compiler_params=pltpu.CompilerParams(vmem_limit_bytes=16 * MIB),
        cost_estimate=pl.CostEstimate(
            flops=2 * n_i * n_k * CHANNELS * 256,
            bytes_accessed=8 * n_i * n_k * CHANNELS,
            transcendentals=2 * n_i * n_k * CHANNELS,
        ),
        name="project_left",
    )(pair, proj, gate)


def right_kernel(own_ref, other_ref, proj_ref, gate_ref, x_out, y_out, turned):
    n_k, n_j, _ = own_ref.shape
    w = both_weights(proj_ref, gate_ref)
    for at, ref in ((0, own_ref), (n_k, other_ref)):
        normed = normed_rows(ref[...]).astype(jnp.bfloat16)
        for k in range(n_k):
            turned[pl.ds(at + k, CHANNELS, stride=2 * n_k), :] = gated(contract_last(w, normed[k]))
    half = CHANNELS // 2
    whole = turned[...].reshape(CHANNELS, 2 * n_k, n_j).astype(jnp.bfloat16)
    x_out[...] = whole[:half]
    y_out[...] = whole[half:]


def project_right(own, other, proj, gate):
    n_k, n_j, _ = own.shape
    half = jax.ShapeDtypeStruct((CHANNELS // 2, 2 * n_k, n_j), jnp.bfloat16)
    return pl.pallas_call(
        right_kernel,
        out_shape=(half, half),
        scratch_shapes=[pltpu.VMEM((CHANNELS * 2 * n_k, n_j), jnp.float32)],
        compiler_params=pltpu.CompilerParams(vmem_limit_bytes=16 * MIB),
        cost_estimate=SHORT,
        name="project_right",
    )(own, other, proj, gate)


def gate_kernel(x_ref, w_ref, o_ref):
    n_i, n_j, _ = x_ref.shape
    normed = normed_rows(x_ref[...]).reshape(n_i * n_j, CHANNELS).astype(jnp.bfloat16)
    logits = jnp.dot(normed, w_ref[...], preferred_element_type=jnp.float32)
    o_ref[...] = jax.nn.sigmoid(logits).reshape(n_i, n_j, CHANNELS).astype(jnp.bfloat16)


def gate_values(pair, weights, at, n_j):
    n_i = pair.shape[0]
    block = 16
    return pl.pallas_call(
        gate_kernel,
        grid=(n_i // block,),
        in_specs=[
            pl.BlockSpec((block, n_j, CHANNELS), lambda s: (s, at, 0)),
            pl.BlockSpec((CHANNELS, CHANNELS), lambda s: (0, 0)),
        ],
        out_specs=pl.BlockSpec((block, n_j, CHANNELS), lambda s: (s, 0, 0)),
        out_shape=jax.ShapeDtypeStruct((n_i, n_j, CHANNELS), jnp.bfloat16),
        compiler_params=pltpu.CompilerParams(vmem_limit_bytes=16 * MIB),
        cost_estimate=SHORT,
        name="gate_values",
    )(pair, weights)


def arrange_kernel(a_ref, b_ref, c_ref, d_ref, order_ref, *rest):
    o_ref = rest[-1]
    order = order_ref[0]
    for ch in range(o_ref.shape[0]):
        rows = jnp.concatenate([a_ref[ch], b_ref[ch], c_ref[ch], d_ref[ch]], axis=0)
        o_ref[ch] = lax.dot_general(
            rows, order, (((0,), (0,)), ((), ())), preferred_element_type=jnp.float32
        ).astype(jnp.bfloat16)


def arrange_left(near, near_core, far, far_core, orders, first, whole=None):
    n_c, n_k, n_i = near.shape
    block = 8
    depth = 4 * n_k
    steps = n_c // 2 // block
    in_specs = (
        [pl.BlockSpec((block, n_k, n_i), lambda s: (s + first * steps, 0, 0))] * 2
        + [pl.BlockSpec((block, n_k, n_i), lambda s: (s, 0, 0))] * 2
        + [pl.BlockSpec((1, depth, depth), lambda s: (first, 0, 0))]
    )
    operands = [near, near_core, far, far_core, orders]
    aliases = {}
    if whole is not None:
        in_specs.append(pl.BlockSpec(memory_space=pl.ANY))
        aliases = {len(operands): 0}
        operands.append(whole)
    return pl.pallas_call(
        arrange_kernel,
        grid=(steps,),
        in_specs=in_specs,
        out_specs=pl.BlockSpec((block, n_i, depth), lambda s: (s + first * steps, 0, 0)),
        out_shape=jax.ShapeDtypeStruct((n_c, n_i, depth), jnp.bfloat16),
        input_output_aliases=aliases,
        compiler_params=pltpu.CompilerParams(vmem_limit_bytes=12 * MIB),
        cost_estimate=SHORT,
        name="arrange_left",
    )(*operands)


def left_orders():
    row, col = lax.axis_index("row"), lax.axis_index("col")
    z_hi, x, y = row // 16, (row // 4) % 4, row % 4
    z_lo, core = col // 2, col % 2
    sign = 1 - 2 * core
    depth = 384
    k = lax.broadcasted_iota(jnp.int32, (depth, depth), 1)
    source = lax.broadcasted_iota(jnp.int32, (depth, depth), 0)
    second, first, z_rel, within = k // 96, (k // 24) % 4, (k // 12) % 2, k % 12
    z_abs = z_hi ^ z_rel

    def order(x_rel, y_rel):
        x_abs = (x - sign * x_rel) % 4
        y_abs = (y - sign * y_rel) % 4
        part = (z_abs ^ z_lo) * 2 + ((x_abs // 2) ^ core)
        return part * 96 + (x_abs % 2) * 48 + y_abs * 12 + within == source

    return jnp.stack([order(first, second), order(second, first)]).astype(jnp.bfloat16)


def update_kernel(n_sum, lx_ref, ly_ref, *refs):
    x_refs, y_refs, (s_ref, w_ref), (o_ref, combined) = refs[:4], refs[4:8], refs[8:10], refs[-2:]
    step = pl.program_id(0)

    @pl.when(step < n_sum)
    def _():
        n_c, n_i, _ = lx_ref.shape
        for at, l_ref, parts in ((0, lx_ref, x_refs), (CHANNELS // 2, ly_ref, y_refs)):
            for ch in range(n_c):
                right = jnp.concatenate([r[ch] for r in parts], axis=0)
                product = jnp.dot(l_ref[ch], right, preferred_element_type=jnp.float32)
                combined[pl.ds(at + step * n_c + ch, n_i, stride=CHANNELS), :] = product

    @pl.when(step >= n_sum)
    def _():
        block = o_ref.shape[0]
        w = w_ref[...]
        first = pl.multiple_of((step - n_sum) * block * CHANNELS, block * CHANNELS)
        for i in range(block):
            values = combined[pl.ds(first + i * CHANNELS, CHANNELS), :]
            average = jnp.mean(values, axis=0, keepdims=True)
            centred = values - average
            variance = jnp.mean(centred * centred, axis=0, keepdims=True)
            normed = (centred * lax.rsqrt(variance + epsilon)).astype(jnp.bfloat16)
            mixed = lax.dot_general(
                normed, w, (((0,), (0,)), ((), ())), preferred_element_type=jnp.float32
            )
            o_ref[i] = (mixed * s_ref[i].astype(jnp.float32)).astype(jnp.bfloat16)


def update_block(left, x_parts, y_parts, gate, weights, at, n_blocks, part, n_parts, whole=None):
    n_c, n_i, depth = left.shape
    half, n_k, n_j = x_parts[0].shape
    c_block, i_block = 16, 32
    rows = n_i // n_parts
    n_sum = half // c_block
    n_out = rows // i_block
    within = lambda s: jnp.minimum(s, n_sum - 1)
    out_at = lambda s: jnp.maximum(s - n_sum, 0) + part * n_out
    in_specs = (
        [
            pl.BlockSpec((c_block, rows, depth), lambda s: (within(s), part, 0)),
            pl.BlockSpec((c_block, rows, depth), lambda s: (within(s) + n_sum, part, 0)),
        ]
        + [pl.BlockSpec((c_block, n_k, n_j), lambda s: (within(s), 0, 0))] * 8
        + [
            pl.BlockSpec((i_block, n_j, CHANNELS), lambda s: (out_at(s), 0, 0)),
            pl.BlockSpec((CHANNELS, CHANNELS), lambda s: (0, 0)),
        ]
    )
    operands = [left, left, *x_parts, *y_parts, gate, weights]
    aliases = {}
    if whole is not None:
        in_specs.append(pl.BlockSpec(memory_space=pl.ANY))
        aliases = {len(operands): 0}
        operands.append(whole)
    return pl.pallas_call(
        functools.partial(update_kernel, n_sum),
        grid=(n_sum + n_out,),
        in_specs=in_specs,
        out_specs=pl.BlockSpec((i_block, n_j, CHANNELS), lambda s: (out_at(s), at, 0)),
        out_shape=jax.ShapeDtypeStruct((n_i, n_blocks * n_j, CHANNELS), jnp.bfloat16),
        scratch_shapes=[pltpu.VMEM((rows * CHANNELS, n_j), jnp.float32)],
        input_output_aliases=aliases,
        compiler_params=pltpu.CompilerParams(vmem_limit_bytes=30 * MIB),
        cost_estimate=SHORT,
        name="update_block",
    )(*operands)


def after(value, *others):
    return lax.optimization_barrier((value, *others))[0]


def step_on(pieces, rings, *others):
    ready = lax.optimization_barrier((*(held[-1] for held in pieces), *others))
    for held, ring, piece in zip(pieces, rings, ready):
        held.append(lax.ppermute(piece, AXES, ring))


def joined(pieces):
    return [[jnp.concatenate(held, axis=1)] for held in pieces]


def shards(
    pair_left,
    pair_right,
    pair_gate,
    left_proj,
    left_gate,
    right_proj,
    right_gate,
    out_gate,
    out_proj,
):
    right = jnp.transpose(pair_right, (1, 0, 2))
    n_j = 128
    n_blocks = right.shape[1] // n_j
    first_rings, second_rings = (RING_X, RING_Y), (RING_Y, RING_X)

    blocks = [right[:, b * n_j : (b + 1) * n_j] for b in range(n_blocks)]
    others = [lax.ppermute(block, AXES, SWAP_Z_HI) for block in blocks]
    left_local = project_left(pair_left, left_proj, left_gate)
    near = [left_local[: CHANNELS // 2], left_local[CHANNELS // 2 :]]
    halves_0 = project_right(blocks[0], after(others[0], left_local), right_proj, right_gate)
    f0 = [[half] for half in halves_0]
    step_on(f0, first_rings)
    halves_1 = project_right(blocks[1], after(others[1], *halves_0), right_proj, right_gate)
    near_core = lax.ppermute(after(left_local, *others, *halves_0), AXES, SWAP_CORE)
    far_0 = lax.ppermute(after(near[0], *halves_1), AXES, SWAP_Z_LO)
    f1 = [[half] for half in halves_1]
    step_on(f1, first_rings)
    step_on(f0, first_rings, *halves_1)
    step_on(f1, first_rings, f0[0][1])
    step_on(f0, first_rings, f1[0][1], f1[1][1], near_core)
    step_on(f1, first_rings, f0[0][2], f0[1][2])

    c0 = joined(f0)
    step_on(c0, second_rings, f1[0][3], f1[1][3])
    c1 = joined(f1)
    step_on(c1, second_rings)
    step_on(c0, second_rings, far_0)
    far_core_0 = lax.ppermute(after(far_0, *[h[3] for h in f1]), AXES, SWAP_CORE)
    far_1 = lax.ppermute(after(near[1], far_0), AXES, SWAP_Z_LO)
    gate_0 = gate_values(pair_gate, after(out_gate, c0[0][1], c0[1][1]), 0, n_j)
    orders = left_orders()
    left = arrange_left(left_local, near_core, far_0, far_core_0, after(orders, gate_0), 0)
    gate_1 = gate_values(pair_gate, after(out_gate, gate_0, c1[0][1], c1[1][1]), 1, n_j)
    step_on(c1, second_rings, gate_1)
    step_on(c0, second_rings)
    far_core_1 = lax.ppermute(after(far_1, c0[0][2], c0[1][2]), AXES, SWAP_CORE)
    left = arrange_left(left_local, near_core, far_1, far_core_1, after(orders, c0[0][2], c0[1][2]), 1, left)
    step_on(c1, second_rings, left)
    whole = update_block(left, *c0, gate_0, out_proj, 0, n_blocks, 0, 1)
    return update_block(left, *c1, gate_1, out_proj, 1, n_blocks, 0, 1, whole)


def solution(mesh):
    placed = (
        P("row", "col", None),
        P("col", "row", None),
        P("row", "col", None),
        P(),
        P(),
        P(),
        P(),
        P(),
        P(),
    )
    return jax.shard_map(
        shards, mesh=mesh, in_specs=placed, out_specs=P("row", "col", None), check_vma=False
    )
```
